32 devices in a mesh: dp: 4 (over z), list: 8 (over y, x, core).
Axes of the slice: x: 2, y: 2, z: 4, core: 2. Of those that a mesh axis runs over, the one named last changes fastest.
Arguments:
- points: bfloat16 [32768, 1024], P(('dp', 'list')), may hold values from -250 to 250
- block_list: int32 [256], P(('dp', 'list')), may hold values from 0 to 3
- centroids: bfloat16 [32, 256, 1024], P('list'), may hold values from -0.5625 to 0.5625
Outputs:
- new_centroids: float32 [32, 256, 1024], P('list', None, 'dp')
- mass: float32 [32, 256], P('list')
The draws below stay inside these ranges and needn't reach their ends.
All inputs are finite; a program needn't handle non-finite values.
Results may differ from the reference program's by a relative error of at most 0.0024.
Values may be sent and summed in bfloat16 or wider, within the bound.
A program may use at most 128 MiB of HBM per device.

```python
import math
import jax
import jax.numpy as jnp
import numpy as np
from jax import lax

D = 1024
CENTS = 256
BLK = 128
SLOT_BLK = 1
LISTS_DEV = 4
LISTS = 32
ROW_BLOCK_TOTAL = 256
POINTS = 32768
N_DP = 4
N_LIST = 8


def draw_points(key, part):
    key = jax.random.fold_in(key, 11)
    first = jax.random.fold_in(key, 0)
    return jnp.clip(jax.random.normal(first, (POINTS, D), jnp.float32), -6.0, 6.0).astype(jnp.bfloat16)


def touch_ends(result, own_key, smallest, high):
    place = [jax.random.randint(jax.random.fold_in(own_key, axis), (), 0, length) for axis, length in enumerate(result.shape)]
    widest = result.shape.index(max(result.shape))
    next_to = place[:widest] + [(place[widest] + 1) % result.shape[widest]] + place[widest + 1:]
    return result.at[tuple(place)].set(smallest).at[tuple(next_to)].set(high)


def shard_levels(key, dims, pieces, smallest, largest):
    def one(dim, parts):
        draws = jax.random.uniform(jax.random.fold_in(jax.random.fold_in(key, 6), dim), (parts,), jnp.float32, smallest / len(pieces), largest / len(pieces))
        return jnp.repeat(jnp.exp(draws), dims[dim] // parts).reshape((-1,) + (1,) * (len(dims) - dim - 1))

    loudness = one(*pieces[0])
    for cut in pieces[1:]:
        loudness = loudness * one(*cut)
    return loudness


def cumulative_ranks(amount, slope):
    loads = [(1 << 20) // math.isqrt(grade ** slope) + 1 for grade in range(1, amount + 1)]
    spread = 1 + sum(loads) // (1 << 30)
    return np.cumsum(np.array([max(1, weight // spread) for weight in loads]))


def ranked(key, dims, amount, slope):
    grid = cumulative_ranks(amount, slope)
    pick = jax.random.randint(jax.random.fold_in(key, 1), dims, 0, int(grid[amount - 1]))
    grade = jnp.searchsorted(jnp.asarray(grid, jnp.int32), pick, side="right")
    return jax.random.permutation(jax.random.fold_in(key, 2), amount)[grade].astype(jnp.int32)


def centred(key, dims, spread, bound, cuts=(), kind=jnp.bfloat16):
    result = spread * jax.random.normal(key, dims, jnp.float32)
    if cuts:
        result = result * shard_levels(key, dims, cuts, -0.22, 0.18)
    return jnp.clip(result, -bound, bound).astype(kind)


def setup_inputs(seed: int = 0) -> dict:
    arg_keys = jax.random.split(jax.random.key(seed), 4)
    return {
        "points": draw_points(jax.random.fold_in(arg_keys[3], 71), 0),
        "block_list": touch_ends(ranked(arg_keys[1], (ROW_BLOCK_TOTAL,), LISTS_DEV, 2), jax.random.fold_in(arg_keys[1], 3), 0, LISTS_DEV - 1).astype(jnp.int32),
        "centroids": centred(arg_keys[2], (LISTS, CENTS, D), (3.0 / D ** 0.5), 0.5625, ((0, 8),)),
    }


def reference(points, block_list, centroids):
    owners = jnp.arange(N_LIST, dtype=jnp.int32)[None, None, :, None] * LISTS_DEV
    lists = (owners + block_list.reshape(N_DP, N_LIST, N_LIST, SLOT_BLK)).astype(jnp.int32).reshape(-1)
    grouped = points.reshape(-1, N_LIST * SLOT_BLK, BLK, D)
    list_groups = lists.reshape(-1, N_LIST * SLOT_BLK)

    def visit(carry, inputs):
        totals, masses = carry
        blocked_rows, chosen_lists = inputs
        picked_lists = centroids[chosen_lists]
        list_scores = jnp.einsum("yif,ysf->yis", blocked_rows.astype(jnp.float32), picked_lists.astype(jnp.float32), precision=lax.Precision.HIGHEST)
        weights = jax.nn.softmax(list_scores, axis=-1).astype(jnp.bfloat16)
        broadened_weights = weights.astype(jnp.float32)
        rows_per_block = jnp.einsum("xes,xez->xsz", broadened_weights, blocked_rows.astype(jnp.float32), precision=lax.Precision.HIGHEST)
        totals = totals.at[chosen_lists].add(rows_per_block)
        masses = masses.at[chosen_lists].add(jnp.sum(broadened_weights, axis=1))
        return (totals, masses), None

    start = (jnp.zeros((LISTS, CENTS, D), jnp.float32), jnp.zeros((LISTS, CENTS), jnp.float32))
    (totals, masses), unused = lax.scan(visit, start, (grouped, list_groups))
    return totals / jnp.maximum(masses, 1.0)[..., None], masses
```

```python
import functools

import jax
import jax.numpy as jnp
from jax import lax
from jax.experimental import pallas as pl
from jax.experimental.pallas import tpu as pltpu
from jax.sharding import PartitionSpec as P

D = 1024
CENTS = 256
BLK = 128
LISTS_DEV = 4
ROWS = LISTS_DEV * CENTS
SPLIT = 2
PART = ROWS // SPLIT
MESH = pl.DeviceIdType.MESH


def exclusive_or(a, b):
    result, bit = 0, 1
    while bit <= b:
        if b & bit:
            result = result + bit - 2 * bit * ((a // bit) % 2)
        bit *= 2
    return a + result


def kernel(
    n, dps, share,
    points, block_list, centroids, totals, mass,
    cents, arrived, list_out, list_in, wts,
    direct_out, far_out, near_in, merge_in, far_in, own_far, mass_out, mass_in,
    local_sem, row_send, row_recv, list_send, list_recv,
    direct_send, far_send, near_recv, merge_recv, far_recv, mass_send, mass_recv,
):
    me = lax.axis_index("list")
    dp = lax.axis_index("dp")
    core = me % 2
    pairs = dps // 2

    cent_copy = pltpu.make_async_copy(centroids, cents, local_sem.at[0])
    cent_copy.start()
    own_copy = pltpu.make_async_copy(points.at[me], arrived.at[0], local_sem.at[1])
    own_copy.start()

    barrier = pltpu.get_barrier_semaphore()
    for k in range(1, n):
        pl.semaphore_signal(barrier, inc=1, device_id={"list": exclusive_or(me, k)}, device_id_type=MESH)
    for k in range(1, dps):
        pl.semaphore_signal(barrier, inc=1, device_id={"dp": (dp + k) % dps}, device_id_type=MESH)
    for o in range(n):
        list_out[o] = jnp.full((1, BLK), block_list[o], jnp.int32)
    list_in[0] = jnp.full((1, BLK), block_list[me], jnp.int32)
    pl.semaphore_wait(barrier, n - 1 + dps - 1)

    def row_copy(i, u):
        k = 2 * i + u
        owner = 2 * exclusive_or(me // 2, i) + (core + u) % 2
        return pltpu.make_async_remote_copy(
            src_ref=points.at[owner], dst_ref=arrived.at[k],
            send_sem=row_send.at[k], recv_sem=row_recv.at[k],
            device_id={"list": owner}, device_id_type=MESH,
        )

    def list_copy(i, u):
        k = 2 * i + u
        owner = 2 * exclusive_or(me // 2, i) + (core + u) % 2
        return pltpu.make_async_remote_copy(
            src_ref=list_out.at[owner], dst_ref=list_in.at[k],
            send_sem=list_send.at[k], recv_sem=list_recv.at[k],
            device_id={"list": owner}, device_id_type=MESH,
        )

    chip_order = list(range(n // 2 - 1, 0, -1))
    for i in range(n // 2):
        for u in range(2):
            if i or u:
                list_copy(i, u).start()
    row_copy(0, 1).start()
    for i in chip_order:
        row_copy(i, core).start()
    for i in chip_order:
        row_copy(i, core).wait_send()
    for i in chip_order:
        row_copy(i, (core + 1) % 2).start()

    def score(k):
        rows = arrived[k]
        lists = list_in[k]
        member = [lists == l for l in range(LISTS_DEV)]
        picked = None
        for l in reversed(range(LISTS_DEV)):
            s = lax.dot_general(cents[l], rows, (((1,), (1,)), ((), ())), preferred_element_type=jnp.float32)
            picked = s if picked is None else jnp.where(member[l], s, picked)
        e = jnp.exp(picked - jnp.max(picked, axis=0, keepdims=True))
        w = e / jnp.sum(e, axis=0, keepdims=True)
        columns = pl.ds(pl.multiple_of(k * BLK, BLK), BLK)
        for l in range(LISTS_DEV):
            wts[l * CENTS:(l + 1) * CENTS, columns] = jnp.where(member[l], w, 0.0).astype(jnp.bfloat16)

    cent_copy.wait()
    own_copy.wait()
    score(0)

    def visit(k, carry):
        i, u = k // 2, k % 2
        pltpu.make_async_remote_copy(
            src_ref=list_out.at[0], dst_ref=list_in.at[k], send_sem=list_send.at[k],
            recv_sem=list_recv.at[k], device_id={"list": me}, device_id_type=MESH,
        ).wait_recv()
        pltpu.make_async_remote_copy(
            src_ref=points.at[0], dst_ref=arrived.at[k], send_sem=row_send.at[k],
            recv_sem=row_recv.at[k], device_id={"list": me}, device_id_type=MESH,
        ).wait_recv()
        score(k)
        return carry

    lax.fori_loop(1, n, visit, 0)

    def partial(d, r):
        columns = pl.ds(pl.multiple_of(d * share, 128), share)
        feats = arrived[:, :, columns].reshape(n * BLK, share)
        return jnp.dot(wts[r * PART:(r + 1) * PART, :], feats, preferred_element_type=jnp.float32)

    partner = dp + 1 - 2 * (dp % 2)
    pair = dp // 2

    def direct_copy(r):
        return pltpu.make_async_remote_copy(
            src_ref=direct_out.at[r], dst_ref=near_in.at[r],
            send_sem=direct_send.at[r], recv_sem=near_recv.at[r],
            device_id={"dp": partner}, device_id_type=MESH,
        )

    def send_direct():
        for r in range(SPLIT):
            direct_out[r] = partial(partner, r).astype(jnp.bfloat16)
            direct_copy(r).start()

    def merge_copy(slot):
        return pltpu.make_async_remote_copy(
            src_ref=far_out.at[slot], dst_ref=merge_in.at[slot],
            send_sem=far_send.at[slot], recv_sem=merge_recv.at[slot],
            device_id={"dp": partner}, device_id_type=MESH,
        )

    def far_copy(slot, dest, landing):
        return pltpu.make_async_remote_copy(
            src_ref=far_out.at[slot], dst_ref=far_in.at[landing],
            send_sem=far_send.at[slot], recv_sem=far_recv.at[landing],
            device_id={"dp": dest}, device_id_type=MESH,
        )

    def mass_copy(k):
        return pltpu.make_async_remote_copy(
            src_ref=mass_out, dst_ref=mass_in.at[k - 1],
            send_sem=mass_send.at[k - 1], recv_sem=mass_recv.at[k - 1],
            device_id={"dp": (dp + k) % dps}, device_id_type=MESH,
        )

    for j in range(1, pairs):
        other = (pair + j) % pairs
        right = (other > pair).astype(jnp.int32)
        outer = (dp + right) % 2 == 1

        @pl.when(outer)
        def _():
            for m in range(2):
                dest = 2 * other + (right + m) % 2
                for r in range(SPLIT):
                    slot = ((j - 1) * 2 + m) * SPLIT + r
                    far_out[slot] = partial(dest, r).astype(jnp.bfloat16)
                    merge_copy(slot).start()

    send_direct()

    lane_mass = lax.dot_general(
        jnp.ones((8, n * BLK), jnp.bfloat16), wts[...], (((1,), (1,)), ((), ())),
        preferred_element_type=jnp.float32,
    )
    for r in range(8):
        mass_out[r:r + 1, :] = lane_mass[r:r + 1, r * 128:(r + 1) * 128]
    for k in range(1, dps):
        mass_copy(k).start()

    for j in range(1, pairs):
        other = (pair + j) % pairs
        right = (other > pair).astype(jnp.int32)
        outer = (dp + right) % 2 == 1

        @pl.when(jnp.logical_not(outer))
        def _():
            for m in range(2):
                dest = 2 * other + (right + m) % 2
                for r in range(SPLIT):
                    own_far[m * SPLIT + r] = partial(dest, r)
            for m in range(2):
                dest = 2 * other + (right + m) % 2
                for r in range(SPLIT):
                    slot = ((j - 1) * 2 + m) * SPLIT + r
                    merge_copy(slot).wait_recv()
                    far_out[slot] = (own_far[m * SPLIT + r] + merge_in[slot].astype(jnp.float32)).astype(jnp.bfloat16)
                    far_copy(slot, dest, (j - 1) * SPLIT + r).start()

    for r in range(SPLIT):
        totals[r * PART:(r + 1) * PART, :] = partial(dp, r)
    for r in range(SPLIT):
        direct_copy(r).wait_recv()
        totals[r * PART:(r + 1) * PART, :] += near_in[r].astype(jnp.float32)
    whole_mass = mass_out[...]
    for k in range(1, dps):
        mass_copy(k).wait_recv()
        whole_mass = whole_mass + mass_in[k - 1]
    mass[...] = whole_mass
    for j in range(1, pairs):
        for r in range(SPLIT):
            landing = (j - 1) * SPLIT + r
            far_copy(landing, partner, landing).wait_recv()
            totals[r * PART:(r + 1) * PART, :] += far_in[landing].astype(jnp.float32)

    for i in range(n // 2):
        for u in range(2):
            if i or u:
                list_copy(i, u).wait_send()
    row_copy(0, 1).wait_send()
    for i in chip_order:
        row_copy(i, (core + 1) % 2).wait_send()
    for r in range(SPLIT):
        direct_copy(r).wait_send()
    for slot in range((pairs - 1) * 2 * SPLIT):
        merge_copy(slot).wait_send()
    for k in range(1, dps):
        mass_copy(k).wait_send()


def on_device(points, block_list, centroids):
    n = lax.axis_size("list")
    dps = lax.axis_size("dp")
    share = D // dps
    pairs = dps // 2
    far = max((pairs - 1) * SPLIT, 1)
    dma = pltpu.SemaphoreType.DMA
    half, single = jnp.bfloat16, jnp.float32
    totals, mass = pl.pallas_call(
        functools.partial(kernel, n, dps, share),
        out_shape=(
            jax.ShapeDtypeStruct((ROWS, share), single),
            jax.ShapeDtypeStruct((8, 128), single),
        ),
        in_specs=[
            pl.BlockSpec(memory_space=pl.ANY),
            pl.BlockSpec(memory_space=pltpu.SMEM),
            pl.BlockSpec(memory_space=pl.ANY),
        ],
        out_specs=(
            pl.BlockSpec(memory_space=pltpu.VMEM),
            pl.BlockSpec(memory_space=pltpu.VMEM),
        ),
        scratch_shapes=[
            pltpu.VMEM((LISTS_DEV, CENTS, D), half),
            pltpu.VMEM((n, BLK, D), half),
            pltpu.VMEM((n, 1, BLK), jnp.int32),
            pltpu.VMEM((n, 1, BLK), jnp.int32),
            pltpu.VMEM((ROWS, n * BLK), half),
            pltpu.VMEM((SPLIT, PART, share), half),
            pltpu.VMEM((2 * far, PART, share), half),
            pltpu.VMEM((SPLIT, PART, share), half),
            pltpu.VMEM((2 * far, PART, share), half),
            pltpu.VMEM((far, PART, share), half),
            pltpu.VMEM((2 * SPLIT, PART, share), single),
            pltpu.VMEM((8, 128), single),
            pltpu.VMEM((dps - 1, 8, 128), single),
            dma((2,)), dma((n,)), dma((n,)), dma((n,)), dma((n,)),
            dma((SPLIT,)), dma((2 * far,)), dma((SPLIT,)), dma((2 * far,)), dma((far,)),
            dma((dps - 1,)), dma((dps - 1,)),
        ],
        compiler_params=pltpu.CompilerParams(
            collective_id=0, has_side_effects=True, vmem_limit_bytes=56 * 1024 * 1024,
        ),
        cost_estimate=pl.CostEstimate(flops=4 * 2 * n * BLK * CENTS * D * 2, bytes_accessed=8 << 20, transcendentals=n * BLK * CENTS),
    )(points.reshape(n, BLK, D), block_list, centroids)
    mass = mass.reshape(LISTS_DEV, CENTS)
    new_centroids = totals.reshape(LISTS_DEV, CENTS, share) / jnp.maximum(mass, 1.0)[..., None]
    return new_centroids, mass


def solution(mesh):
    placed = (P(("dp", "list"), None), P(("dp", "list")), P("list", None, None))
    return jax.shard_map(
        on_device,
        mesh=mesh,
        in_specs=placed,
        out_specs=(P("list", None, "dp"), P("list", None)),
        check_vma=False,
    )
```

```python
import functools

import jax
import jax.numpy as jnp
from jax import lax
from jax.experimental import pallas as pl
from jax.experimental.pallas import tpu as pltpu
from jax.sharding import PartitionSpec as P

D = 1024
CENTS = 256
BLK = 128
LISTS_DEV = 4
ROWS = LISTS_DEV * CENTS
SPLIT = 2
PART = ROWS // SPLIT
MESH = pl.DeviceIdType.MESH


def exclusive_or(a, b):
    result, bit = 0, 1
    while bit <= b:
        if b & bit:
            result = result + bit - 2 * bit * ((a // bit) % 2)
        bit *= 2
    return a + result


def kernel(
    n, dps, share,
    points, block_list, centroids, totals, mass,
    cents, arrived, list_out, list_in, wts,
    direct_out, far_out, near_in, merge_in, far_in, own_far, mass_out, mass_in,
    local_sem, row_send, row_recv, list_send, list_recv,
    direct_send, far_send, near_recv, merge_recv, far_recv, mass_send, mass_recv,
):
    me = lax.axis_index("list")
    dp = lax.axis_index("dp")
    core, chip = me % 2, me // 2
    chips = n // 2
    pairs = dps // 2
    pair = dp // 2
    partner = dp + 1 - 2 * (dp % 2)

    def home_of(p):
        return 2 * p + (2 * p < pairs).astype(jnp.int32)

    home = home_of(pair)
    away = (dp != home).astype(jnp.int32)
    even = core == 0
    gathers = (core == 1) & (away == 0)
    idle = (core == 1) & (away == 1)

    cent_copy = pltpu.make_async_copy(centroids, cents, local_sem.at[0])
    cent_copy.start()
    own_copy = pltpu.make_async_copy(points.at[me], arrived.at[0], local_sem.at[1])

    @pl.when(jnp.logical_not(idle))
    def _():
        own_copy.start()

    barrier = pltpu.get_barrier_semaphore()
    for k in range(1, n):
        peer = exclusive_or(me, k)
        pl.semaphore_signal(barrier, inc=1, device_id={"dp": dp, "list": peer}, device_id_type=MESH)
        pl.semaphore_signal(barrier, inc=1, device_id={"dp": partner, "list": peer}, device_id_type=MESH)
    for k in range(1, dps):
        pl.semaphore_signal(barrier, inc=1, device_id={"dp": (dp + k) % dps, "list": me}, device_id_type=MESH)
    for o in range(n):
        list_out[o] = jnp.full((1, BLK), block_list[o], jnp.int32)
    list_in[0] = jnp.full((1, BLK), block_list[me], jnp.int32)
    pl.semaphore_wait(barrier, 2 * (n - 1) + dps - 1)

    def route(i, odd):
        k = 2 * i + (core + odd) % 2
        owner = 2 * exclusive_or(chip, i) + odd
        target = dp + odd * (home - dp)
        return k, owner, target, k + n * odd * away

    def row_copy(i, odd):
        k, owner, target, slot = route(i, odd)
        return pltpu.make_async_remote_copy(
            src_ref=points.at[owner], dst_ref=arrived.at[slot],
            send_sem=row_send.at[k], recv_sem=row_recv.at[slot],
            device_id={"dp": target, "list": owner}, device_id_type=MESH,
        )

    def list_copy(i, odd):
        k, owner, target, slot = route(i, odd)
        return pltpu.make_async_remote_copy(
            src_ref=list_out.at[owner], dst_ref=list_in.at[slot],
            send_sem=list_send.at[k], recv_sem=list_recv.at[slot],
            device_id={"dp": target, "list": owner}, device_id_type=MESH,
        )

    def each_route(act):
        for i in range(chips):
            for odd in (away, 1 - away):
                if i:
                    act(i, odd)
                else:
                    @pl.when((core != odd) | (odd * away == 1))
                    def _():
                        act(i, odd)

    each_route(lambda i, odd: list_copy(i, odd).start())
    each_route(lambda i, odd: row_copy(i, odd).start())

    def score(batch):
        rows = arrived[pl.ds(2 * batch, 2)].reshape(2 * BLK, D)
        lists = jnp.concatenate([list_in[2 * batch], list_in[2 * batch + 1]], axis=1)
        member = [lists == l for l in range(LISTS_DEV)]
        picked = None
        for l in reversed(range(LISTS_DEV)):
            s = lax.dot_general(cents[l], rows, (((1,), (1,)), ((), ())), preferred_element_type=jnp.float32)
            picked = s if picked is None else jnp.where(member[l], s, picked)
        e = jnp.exp(picked - jnp.max(picked, axis=0, keepdims=True))
        w = e / jnp.sum(e, axis=0, keepdims=True)
        columns = pl.ds(pl.multiple_of(batch * 2 * BLK, 2 * BLK), 2 * BLK)
        for l in range(LISTS_DEV):
            wts[l * CENTS:(l + 1) * CENTS, columns] = jnp.where(member[l], w, 0.0).astype(jnp.bfloat16)

    def landed(slot):
        pltpu.make_async_remote_copy(
            src_ref=list_out.at[0], dst_ref=list_in.at[slot], send_sem=list_send.at[0],
            recv_sem=list_recv.at[slot], device_id={"dp": dp, "list": me}, device_id_type=MESH,
        ).wait_recv()
        pltpu.make_async_remote_copy(
            src_ref=points.at[0], dst_ref=arrived.at[slot], send_sem=row_send.at[0],
            recv_sem=row_recv.at[slot], device_id={"dp": dp, "list": me}, device_id_type=MESH,
        ).wait_recv()

    cent_copy.wait()

    @pl.when(jnp.logical_not(idle))
    def _():
        own_copy.wait()
        landed(1)
        score(0)

        def visit(step, carry):
            batch = step + (core * ((step // 2) + (step % 2) * chips - step))
            landed(2 * batch)
            landed(2 * batch + 1)
            score(batch)
            return carry

        lax.fori_loop(1, chips * (1 + core), visit, 0)

    def partial(d, r, count):
        columns = pl.ds(pl.multiple_of(d * share, 128), share)
        feats = arrived[0:count, :, columns].reshape(count * BLK, share)
        return jnp.dot(
            wts[r * PART:(r + 1) * PART, 0:count * BLK], feats, preferred_element_type=jnp.float32
        )

    def direct_copy(r):
        return pltpu.make_async_remote_copy(
            src_ref=direct_out.at[r], dst_ref=near_in.at[r],
            send_sem=direct_send.at[r], recv_sem=near_recv.at[r],
            device_id={"dp": partner, "list": me}, device_id_type=MESH,
        )

    def send_direct(count):
        for r in range(SPLIT):
            direct_out[r] = partial(partner, r, count).astype(jnp.bfloat16)
            direct_copy(r).start()

    def merge_copy(slot):
        return pltpu.make_async_remote_copy(
            src_ref=far_out.at[slot], dst_ref=merge_in.at[slot],
            send_sem=far_send.at[slot], recv_sem=merge_recv.at[slot],
            device_id={"dp": partner, "list": me}, device_id_type=MESH,
        )

    def far_copy(slot, dest, landing):
        return pltpu.make_async_remote_copy(
            src_ref=far_out.at[slot], dst_ref=far_in.at[landing],
            send_sem=far_send.at[slot], recv_sem=far_recv.at[landing],
            device_id={"dp": dest, "list": me}, device_id_type=MESH,
        )

    def mass_copy(k):
        return pltpu.make_async_remote_copy(
            src_ref=mass_out, dst_ref=mass_in.at[k - 1],
            send_sem=mass_send.at[k - 1], recv_sem=mass_recv.at[k - 1],
            device_id={"dp": (dp + k) % dps, "list": me}, device_id_type=MESH,
        )

    def send_mass(count):
        lane_mass = lax.dot_general(
            jnp.ones((8, count * BLK), jnp.bfloat16), wts[:, 0:count * BLK], (((1,), (1,)), ((), ())),
            preferred_element_type=jnp.float32,
        )
        for r in range(8):
            mass_out[r:r + 1, :] = lane_mass[r:r + 1, r * 128:(r + 1) * 128]
        for k in range(1, dps):
            mass_copy(k).start()

    def others():
        for j in range(1, pairs):
            other = (pair + j) % pairs
            right = (other > pair).astype(jnp.int32)
            yield j, other, right, (dp + right) % 2 == 1

    def far_parts(j, other, right):
        for m in range(2):
            for r in range(SPLIT):
                yield 2 * other + (right + m) % 2, m, r, ((j - 1) * 2 + m) * SPLIT + r

    @pl.when(even)
    def _():
        for j, other, right, outer in others():
            @pl.when(outer)
            def _():
                for dest, m, r, slot in far_parts(j, other, right):
                    far_out[slot] = partial(dest, r, n).astype(jnp.bfloat16)
                    merge_copy(slot).start()

        send_direct(n)
        send_mass(n)

        for j, other, right, outer in others():
            @pl.when(jnp.logical_not(outer))
            def _():
                for dest, m, r, slot in far_parts(j, other, right):
                    own_far[m * SPLIT + r] = partial(dest, r, n)
                for dest, m, r, slot in far_parts(j, other, right):
                    merge_copy(slot).wait_recv()
                    far_out[slot] = (own_far[m * SPLIT + r] + merge_in[slot].astype(jnp.float32)).astype(jnp.bfloat16)
                    far_copy(slot, dest, (j - 1) * SPLIT + r).start()

        for r in range(SPLIT):
            totals[r * PART:(r + 1) * PART, :] = partial(dp, r, n)

    @pl.when(gathers)
    def _():
        for j, other, right, outer in others():
            for dest, m, r, slot in far_parts(j, other, right):
                far_out[slot] = partial(dest, r, 2 * n).astype(jnp.bfloat16)
                far_copy(slot, dest, (j - 1) * SPLIT + r).start()
        send_direct(2 * n)
        send_mass(2 * n)
        for r in range(SPLIT):
            totals[r * PART:(r + 1) * PART, :] = partial(dp, r, 2 * n)

    @pl.when(idle)
    def _():
        totals[...] = jnp.zeros_like(totals)
        mass_out[...] = jnp.zeros_like(mass_out)

    mass[...] = mass_out[...]
    for k in range(1, dps):
        sender = (dp + dps - k) % dps

        @pl.when(even | (sender == home_of(sender // 2)))
        def _():
            mass_copy(k).wait_recv()
            mass[...] += mass_in[k - 1]

    for j in range(1, pairs):
        for r in range(SPLIT):
            landing = (j - 1) * SPLIT + r
            far_copy(landing, partner, landing).wait_recv()
            totals[r * PART:(r + 1) * PART, :] += far_in[landing].astype(jnp.float32)

    @pl.when(jnp.logical_not(gathers))
    def _():
        for r in range(SPLIT):
            direct_copy(r).wait_recv()
            totals[r * PART:(r + 1) * PART, :] += near_in[r].astype(jnp.float32)

    each_route(lambda i, odd: list_copy(i, odd).wait_send())
    each_route(lambda i, odd: row_copy(i, odd).wait_send())

    @pl.when(jnp.logical_not(idle))
    def _():
        for r in range(SPLIT):
            direct_copy(r).wait_send()
        for slot in range((pairs - 1) * 2 * SPLIT):
            merge_copy(slot).wait_send()
        for k in range(1, dps):
            mass_copy(k).wait_send()


def on_device(points, block_list, centroids):
    n = lax.axis_size("list")
    dps = lax.axis_size("dp")
    share = D // dps
    pairs = dps // 2
    far = max((pairs - 1) * SPLIT, 1)
    dma = pltpu.SemaphoreType.DMA
    half, single = jnp.bfloat16, jnp.float32
    totals, mass = pl.pallas_call(
        functools.partial(kernel, n, dps, share),
        out_shape=(
            jax.ShapeDtypeStruct((ROWS, share), single),
            jax.ShapeDtypeStruct((8, 128), single),
        ),
        in_specs=[
            pl.BlockSpec(memory_space=pl.ANY),
            pl.BlockSpec(memory_space=pltpu.SMEM),
            pl.BlockSpec(memory_space=pl.ANY),
        ],
        out_specs=(
            pl.BlockSpec(memory_space=pltpu.VMEM),
            pl.BlockSpec(memory_space=pltpu.VMEM),
        ),
        scratch_shapes=[
            pltpu.VMEM((LISTS_DEV, CENTS, D), half),
            pltpu.VMEM((2 * n, BLK, D), half),
            pltpu.VMEM((n, 1, BLK), jnp.int32),
            pltpu.VMEM((2 * n, 1, BLK), jnp.int32),
            pltpu.VMEM((ROWS, 2 * n * BLK), half),
            pltpu.VMEM((SPLIT, PART, share), half),
            pltpu.VMEM((2 * far, PART, share), half),
            pltpu.VMEM((SPLIT, PART, share), half),
            pltpu.VMEM((2 * far, PART, share), half),
            pltpu.VMEM((far, PART, share), half),
            pltpu.VMEM((2 * SPLIT, PART, share), single),
            pltpu.VMEM((8, 128), single),
            pltpu.VMEM((dps - 1, 8, 128), single),
            dma((2,)), dma((n,)), dma((2 * n,)), dma((n,)), dma((2 * n,)),
            dma((SPLIT,)), dma((2 * far,)), dma((SPLIT,)), dma((2 * far,)), dma((far,)),
            dma((dps - 1,)), dma((dps - 1,)),
        ],
        compiler_params=pltpu.CompilerParams(
            collective_id=0, has_side_effects=True, vmem_limit_bytes=56 * 1024 * 1024,
        ),
        cost_estimate=pl.CostEstimate(flops=4 * 2 * n * BLK * CENTS * D * 2, bytes_accessed=8 << 20, transcendentals=n * BLK * CENTS),
    )(points.reshape(n, BLK, D), block_list, centroids)
    mass = mass.reshape(LISTS_DEV, CENTS)
    new_centroids = totals.reshape(LISTS_DEV, CENTS, share) / jnp.maximum(mass, 1.0)[..., None]
    return new_centroids, mass


def solution(mesh):
    placed = (P(("dp", "list"), None), P(("dp", "list")), P("list", None, None))
    return jax.shard_map(
        on_device,
        mesh=mesh,
        in_specs=placed,
        out_specs=(P("list", None, "dp"), P("list", None)),
        check_vma=False,
    )
```

```python
import functools

import jax
import jax.numpy as jnp
from jax import lax
from jax.experimental import pallas as pl
from jax.experimental.pallas import tpu as pltpu
from jax.sharding import PartitionSpec as P

D = 1024
CENTS = 256
BLK = 128
LISTS_DEV = 4
ROWS = LISTS_DEV * CENTS
SPLIT = 2
PART = ROWS // SPLIT
MESH = pl.DeviceIdType.MESH


def exclusive_or(a, b):
    result, bit = 0, 1
    while bit <= b:
        if b & bit:
            result = result + bit - 2 * bit * ((a // bit) % 2)
        bit *= 2
    return a + result


def kernel(
    n, dps, share,
    points, block_list, centroids, totals, mass,
    cents, arrived, list_out, list_in, wts,
    direct_out, far_out, near_in, merge_in, far_in, own_far, mass_out, mass_in,
    local_sem, row_send, row_recv, list_send, list_recv, pass_send, pass_list_send,
    direct_send, far_send, near_recv, merge_recv, far_recv, mass_send, mass_recv,
):
    me = lax.axis_index("list")
    dp = lax.axis_index("dp")
    core, chip = me % 2, me // 2
    chips = n // 2
    pairs = dps // 2
    pair = dp // 2
    partner = dp + 1 - 2 * (dp % 2)

    def home_of(p):
        return 2 * p + (2 * p < pairs).astype(jnp.int32)

    home = home_of(pair)
    away = (dp != home).astype(jnp.int32)
    even = core == 0
    gathers = (core == 1) & (away == 0)
    idle = (core == 1) & (away == 1)

    cent_copy = pltpu.make_async_copy(centroids, cents, local_sem.at[0])
    cent_copy.start()
    own_copy = pltpu.make_async_copy(points.at[me], arrived.at[0], local_sem.at[1])

    @pl.when(jnp.logical_not(idle))
    def _():
        own_copy.start()

    barrier = pltpu.get_barrier_semaphore()
    for k in range(1, n):
        peer = exclusive_or(me, k)
        pl.semaphore_signal(barrier, inc=1, device_id={"dp": dp, "list": peer}, device_id_type=MESH)
    for k in range(1, dps):
        pl.semaphore_signal(barrier, inc=1, device_id={"dp": (dp + k) % dps, "list": me}, device_id_type=MESH)
    for o in range(n):
        list_out[o] = jnp.full((1, BLK), block_list[o], jnp.int32)
    list_in[0] = jnp.full((1, BLK), block_list[me], jnp.int32)
    pl.semaphore_wait(barrier, n - 1 + dps - 1)

    def route(i, odd):
        k = 2 * i + (core + odd) % 2
        owner = 2 * exclusive_or(chip, i) + odd
        return k, owner

    def row_copy(i, odd):
        k, owner = route(i, odd)
        return pltpu.make_async_remote_copy(
            src_ref=points.at[owner], dst_ref=arrived.at[k],
            send_sem=row_send.at[k], recv_sem=row_recv.at[k],
            device_id={"dp": dp, "list": owner}, device_id_type=MESH,
        )

    def list_copy(i, odd):
        k, owner = route(i, odd)
        return pltpu.make_async_remote_copy(
            src_ref=list_out.at[owner], dst_ref=list_in.at[k],
            send_sem=list_send.at[k], recv_sem=list_recv.at[k],
            device_id={"dp": dp, "list": owner}, device_id_type=MESH,
        )

    def each_route(act):
        for i in range(chips):
            for odd in (away, 1 - away):
                if i:
                    act(i, odd)
                else:
                    @pl.when(core != odd)
                    def _():
                        act(i, odd)

    def forward_rows(k, source):
        return pltpu.make_async_remote_copy(
            src_ref=source, dst_ref=arrived.at[n + k],
            send_sem=pass_send.at[k], recv_sem=row_recv.at[n + k],
            device_id={"dp": partner, "list": me}, device_id_type=MESH,
        )

    def forward_list(k):
        return pltpu.make_async_remote_copy(
            src_ref=list_in.at[k], dst_ref=list_in.at[n + k],
            send_sem=pass_list_send.at[k], recv_sem=list_recv.at[n + k],
            device_id={"dp": partner, "list": me}, device_id_type=MESH,
        )

    @pl.when(idle)
    def _():
        forward_list(0).start()
        forward_rows(0, points.at[me]).start()

    each_route(lambda i, odd: list_copy(i, odd).start())
    each_route(lambda i, odd: row_copy(i, odd).start())

    def score(batch):
        rows = arrived[pl.ds(2 * batch, 2)].reshape(2 * BLK, D)
        lists = jnp.concatenate([list_in[2 * batch], list_in[2 * batch + 1]], axis=1)
        member = [lists == l for l in range(LISTS_DEV)]
        picked = None
        for l in reversed(range(LISTS_DEV)):
            s = lax.dot_general(cents[l], rows, (((1,), (1,)), ((), ())), preferred_element_type=jnp.float32)
            picked = s if picked is None else jnp.where(member[l], s, picked)
        e = jnp.exp(picked - jnp.max(picked, axis=0, keepdims=True))
        w = e / jnp.sum(e, axis=0, keepdims=True)
        columns = pl.ds(pl.multiple_of(batch * 2 * BLK, 2 * BLK), 2 * BLK)
        for l in range(LISTS_DEV):
            wts[l * CENTS:(l + 1) * CENTS, columns] = jnp.where(member[l], w, 0.0).astype(jnp.bfloat16)

    def landed(slot):
        pltpu.make_async_remote_copy(
            src_ref=list_out.at[0], dst_ref=list_in.at[slot], send_sem=list_send.at[0],
            recv_sem=list_recv.at[slot], device_id={"dp": dp, "list": me}, device_id_type=MESH,
        ).wait_recv()
        pltpu.make_async_remote_copy(
            src_ref=points.at[0], dst_ref=arrived.at[slot], send_sem=row_send.at[0],
            recv_sem=row_recv.at[slot], device_id={"dp": dp, "list": me}, device_id_type=MESH,
        ).wait_recv()

    cent_copy.wait()

    @pl.when(idle)
    def _():
        def pass_on(k, carry):
            landed(k)
            forward_list(k).start()
            forward_rows(k, arrived.at[k]).start()
            return carry

        lax.fori_loop(1, n, pass_on, 0)

    @pl.when(jnp.logical_not(idle))
    def _():
        own_copy.wait()
        landed(1)
        score(0)

        def visit(step, carry):
            batch = step + (core * ((step // 2) + (step % 2) * chips - step))
            landed(2 * batch)
            landed(2 * batch + 1)
            score(batch)
            return carry

        lax.fori_loop(1, chips * (1 + core), visit, 0)

    def partial(d, r, count):
        columns = pl.ds(pl.multiple_of(d * share, 128), share)
        feats = arrived[0:count, :, columns].reshape(count * BLK, share)
        return jnp.dot(
            wts[r * PART:(r + 1) * PART, 0:count * BLK], feats, preferred_element_type=jnp.float32
        )

    def direct_copy(r):
        return pltpu.make_async_remote_copy(
            src_ref=direct_out.at[r], dst_ref=near_in.at[r],
            send_sem=direct_send.at[r], recv_sem=near_recv.at[r],
            device_id={"dp": partner, "list": me}, device_id_type=MESH,
        )

    def send_direct(count):
        for r in range(SPLIT):
            direct_out[r] = partial(partner, r, count).astype(jnp.bfloat16)
            direct_copy(r).start()

    def merge_copy(slot):
        return pltpu.make_async_remote_copy(
            src_ref=far_out.at[slot], dst_ref=merge_in.at[slot],
            send_sem=far_send.at[slot], recv_sem=merge_recv.at[slot],
            device_id={"dp": partner, "list": me}, device_id_type=MESH,
        )

    def far_copy(slot, dest, landing):
        return pltpu.make_async_remote_copy(
            src_ref=far_out.at[slot], dst_ref=far_in.at[landing],
            send_sem=far_send.at[slot], recv_sem=far_recv.at[landing],
            device_id={"dp": dest, "list": me}, device_id_type=MESH,
        )

    def mass_copy(k):
        return pltpu.make_async_remote_copy(
            src_ref=mass_out, dst_ref=mass_in.at[k - 1],
            send_sem=mass_send.at[k - 1], recv_sem=mass_recv.at[k - 1],
            device_id={"dp": (dp + k) % dps, "list": me}, device_id_type=MESH,
        )

    def send_mass(count):
        lane_mass = lax.dot_general(
            jnp.ones((8, count * BLK), jnp.bfloat16), wts[:, 0:count * BLK], (((1,), (1,)), ((), ())),
            preferred_element_type=jnp.float32,
        )
        for r in range(8):
            mass_out[r:r + 1, :] = lane_mass[r:r + 1, r * 128:(r + 1) * 128]
        for k in range(1, dps):
            mass_copy(k).start()

    def others():
        for j in range(1, pairs):
            other = (pair + j) % pairs
            right = (other > pair).astype(jnp.int32)
            yield j, other, right, (dp + right) % 2 == 1

    def far_parts(j, other, right):
        for m in range(2):
            for r in range(SPLIT):
                yield 2 * other + (right + m) % 2, m, r, ((j - 1) * 2 + m) * SPLIT + r

    @pl.when(even)
    def _():
        for j, other, right, outer in others():
            @pl.when(outer)
            def _():
                for dest, m, r, slot in far_parts(j, other, right):
                    far_out[slot] = partial(dest, r, n).astype(jnp.bfloat16)
                    merge_copy(slot).start()

        send_direct(n)
        send_mass(n)

        for j, other, right, outer in others():
            @pl.when(jnp.logical_not(outer))
            def _():
                for dest, m, r, slot in far_parts(j, other, right):
                    own_far[m * SPLIT + r] = partial(dest, r, n)
                for dest, m, r, slot in far_parts(j, other, right):
                    merge_copy(slot).wait_recv()
                    far_out[slot] = (own_far[m * SPLIT + r] + merge_in[slot].astype(jnp.float32)).astype(jnp.bfloat16)
                    far_copy(slot, dest, (j - 1) * SPLIT + r).start()

        for r in range(SPLIT):
            totals[r * PART:(r + 1) * PART, :] = partial(dp, r, n)

    @pl.when(gathers)
    def _():
        for j, other, right, outer in others():
            for dest, m, r, slot in far_parts(j, other, right):
                far_out[slot] = partial(dest, r, 2 * n).astype(jnp.bfloat16)
                far_copy(slot, dest, (j - 1) * SPLIT + r).start()
        send_direct(2 * n)
        send_mass(2 * n)
        for r in range(SPLIT):
            totals[r * PART:(r + 1) * PART, :] = partial(dp, r, 2 * n)

    @pl.when(idle)
    def _():
        totals[...] = jnp.zeros_like(totals)
        mass_out[...] = jnp.zeros_like(mass_out)

        def passed(k, carry):
            forward_list(k).wait_send()
            forward_rows(k, points.at[me]).wait_send()
            return carry

        lax.fori_loop(0, n, passed, 0)

    mass[...] = mass_out[...]
    for k in range(1, dps):
        sender = (dp + dps - k) % dps

        @pl.when(even | (sender == home_of(sender // 2)))
        def _():
            mass_copy(k).wait_recv()
            mass[...] += mass_in[k - 1]

    for j in range(1, pairs):
        for r in range(SPLIT):
            landing = (j - 1) * SPLIT + r
            far_copy(landing, partner, landing).wait_recv()
            totals[r * PART:(r + 1) * PART, :] += far_in[landing].astype(jnp.float32)

    @pl.when(jnp.logical_not(gathers))
    def _():
        for r in range(SPLIT):
            direct_copy(r).wait_recv()
            totals[r * PART:(r + 1) * PART, :] += near_in[r].astype(jnp.float32)

    each_route(lambda i, odd: list_copy(i, odd).wait_send())
    each_route(lambda i, odd: row_copy(i, odd).wait_send())

    @pl.when(jnp.logical_not(idle))
    def _():
        for r in range(SPLIT):
            direct_copy(r).wait_send()
        for slot in range((pairs - 1) * 2 * SPLIT):
            merge_copy(slot).wait_send()
        for k in range(1, dps):
            mass_copy(k).wait_send()


def on_device(points, block_list, centroids):
    n = lax.axis_size("list")
    dps = lax.axis_size("dp")
    share = D // dps
    pairs = dps // 2
    far = max((pairs - 1) * SPLIT, 1)
    dma = pltpu.SemaphoreType.DMA
    half, single = jnp.bfloat16, jnp.float32
    totals, mass = pl.pallas_call(
        functools.partial(kernel, n, dps, share),
        out_shape=(
            jax.ShapeDtypeStruct((ROWS, share), single),
            jax.ShapeDtypeStruct((8, 128), single),
        ),
        in_specs=[
            pl.BlockSpec(memory_space=pl.ANY),
            pl.BlockSpec(memory_space=pltpu.SMEM),
            pl.BlockSpec(memory_space=pl.ANY),
        ],
        out_specs=(
            pl.BlockSpec(memory_space=pltpu.VMEM),
            pl.BlockSpec(memory_space=pltpu.VMEM),
        ),
        scratch_shapes=[
            pltpu.VMEM((LISTS_DEV, CENTS, D), half),
            pltpu.VMEM((2 * n, BLK, D), half),
            pltpu.VMEM((n, 1, BLK), jnp.int32),
            pltpu.VMEM((2 * n, 1, BLK), jnp.int32),
            pltpu.VMEM((ROWS, 2 * n * BLK), half),
            pltpu.VMEM((SPLIT, PART, share), half),
            pltpu.VMEM((2 * far, PART, share), half),
            pltpu.VMEM((SPLIT, PART, share), half),
            pltpu.VMEM((2 * far, PART, share), half),
            pltpu.VMEM((far, PART, share), half),
            pltpu.VMEM((2 * SPLIT, PART, share), single),
            pltpu.VMEM((8, 128), single),
            pltpu.VMEM((dps - 1, 8, 128), single),
            dma((2,)), dma((n,)), dma((2 * n,)), dma((n,)), dma((2 * n,)), dma((n,)), dma((n,)),
            dma((SPLIT,)), dma((2 * far,)), dma((SPLIT,)), dma((2 * far,)), dma((far,)),
            dma((dps - 1,)), dma((dps - 1,)),
        ],
        compiler_params=pltpu.CompilerParams(
            collective_id=0, has_side_effects=True, vmem_limit_bytes=56 * 1024 * 1024,
        ),
        cost_estimate=pl.CostEstimate(flops=4 * 2 * n * BLK * CENTS * D * 2, bytes_accessed=8 << 20, transcendentals=n * BLK * CENTS),
    )(points.reshape(n, BLK, D), block_list, centroids)
    mass = mass.reshape(LISTS_DEV, CENTS)
    new_centroids = totals.reshape(LISTS_DEV, CENTS, share) / jnp.maximum(mass, 1.0)[..., None]
    return new_centroids, mass


def solution(mesh):
    placed = (P(("dp", "list"), None), P(("dp", "list")), P("list", None, None))
    return jax.shard_map(
        on_device,
        mesh=mesh,
        in_specs=placed,
        out_specs=(P("list", None, "dp"), P("list", None)),
        check_vma=False,
    )
```
